512 devices in a mesh: dp: 4 (over x), row: 8 (over y, core), col: 16 (over z).
Axes of the slice: x: 4, y: 4, z: 16, core: 2. Of those that a mesh axis runs over, the one named last changes fastest.
Arguments:
- tokens: bfloat16 [512, 4608], P(('dp', 'col'), 'row'), may hold values from -6 to 6
- w_gate: bfloat16 [4608, 24576], P('row', ('dp', 'col')), may hold values from -0.09375 to 0.09375
- w_up: bfloat16 [4608, 24576], P('row', ('dp', 'col')), may hold values from -0.09375 to 0.09375
- w_down: bfloat16 [24576, 4608], P(('dp', 'col'), 'row'), may hold values from -0.0390625 to 0.0390625
- g_gate: bfloat16 [4608, 24576], P('row', ('dp', 'col')), may hold values from -6000 to 6000
- g_up: bfloat16 [4608, 24576], P('row', ('dp', 'col')), may hold values from -6000 to 6000
- g_down: bfloat16 [24576, 4608], P(('dp', 'col'), 'row'), may hold values from -6000 to 6000
- cotangent: bfloat16 [512, 4608], P(('dp', 'col'), 'row'), may hold values from -6 to 6
Outputs:
- grad_tokens: bfloat16 [512, 4608], P(('dp', 'col'), 'row')
- grad_gate: bfloat16 [4608, 24576], P('row', ('dp', 'col'))
- grad_up: bfloat16 [4608, 24576], P('row', ('dp', 'col'))
- grad_down: bfloat16 [24576, 4608], P(('dp', 'col'), 'row')
The draws below stay inside these ranges and needn't reach their ends.
All inputs are finite; a program needn't handle non-finite values.
Results may differ from the reference program's by a relative error of at most 0.0073.
Values may be sent and summed in bfloat16 or wider, within the bound.
No kernel may reach another device: no remote copies, remote signals or barrier semaphores. Data moves between devices by JAX's collectives and lax.ppermute only.
A program may use at most 64 MiB of HBM per device.

```python
import math
import jax
import jax.numpy as jnp

D = 4608
FF = 24576
TOKENS = 512


def scaled_field(base, key, span):
    nrows = base.shape[0]
    ncols = base.shape[1]
    key_rows, key_cols = jax.random.split(key)
    row_scale = jnp.exp(jax.random.uniform(key_rows, (nrows, 1), jnp.float32, 0.0, math.log(span)))
    row_scale = row_scale * 3.0 ** (jnp.arange(nrows, dtype=jnp.float32)[:, None] / nrows)
    col_scale = jnp.exp(jax.random.uniform(key_cols, (1, ncols), jnp.float32, 0.0, math.log(span)))
    col_scale = col_scale * 3.0 ** (jnp.arange(ncols, dtype=jnp.float32)[None, :] / ncols)
    return (base * row_scale * col_scale).astype(jnp.bfloat16)


def draw_g_gate(key, part):
    key = jax.random.fold_in(key, 11)
    key_base, key_scale = jax.random.split(key)
    base = jnp.clip(jax.random.normal(key_base, (D, FF), jnp.float32), -4.0, 4.0)
    return scaled_field(base, key_scale, 10.0)


def draw_g_up(key, part):
    key = jax.random.fold_in(key, 23)
    key_base, key_scale = jax.random.split(key)
    base = jnp.clip(jax.random.normal(key_base, (D, FF), jnp.float32), -4.0, 4.0)
    return scaled_field(base, key_scale, 10.0)


def draw_g_down(key, part):
    key = jax.random.fold_in(key, 37)
    key_base, key_scale = jax.random.split(key)
    base = jnp.clip(jax.random.normal(key_base, (FF, D), jnp.float32), -4.0, 4.0)
    return scaled_field(base, key_scale, 10.0)


def shard_levels(stream_key, dims, shards, low, top_value):
    level, own = 1.0, jax.random.fold_in(stream_key, 6)
    for dim, blocks in shards:
        heights = jnp.exp(jax.random.uniform(jax.random.fold_in(own, dim), (blocks,), jnp.float32, low / len(shards), top_value / len(shards)))
        level = level * jnp.repeat(heights, dims[dim] // blocks).reshape([-1 if axis == dim else 1 for axis in range(len(dims))])
    return level


def noise(key, shape, scale, limit, cuts=(), held_as=jnp.bfloat16):
    entries = jax.random.normal(key, shape, jnp.float32) * scale
    if len(cuts) > 0:
        entries = shard_levels(key, shape, cuts, -0.22, 0.18) * entries
    return jnp.clip(entries, min=-limit, max=limit).astype(held_as)


def setup_inputs(seed: int = 0) -> dict:
    splits = jax.random.split(jax.random.key(seed), 9)
    tokens = noise(splits[0], (TOKENS, D), 1.0, 6.0, ((0, 64), (1, 8)))
    w_gate = noise(splits[1], (D, FF), D ** -0.5, 0.09375, ((0, 8), (1, 64)))
    w_up = noise(splits[2], (D, FF), D ** -0.5, 0.09375, ((0, 8), (1, 64)))
    w_down = noise(splits[3], (FF, D), FF ** -0.5, 0.0390625, ((0, 64), (1, 8)))
    g_gate = draw_g_gate(jax.random.fold_in(splits[8], 71), 0)
    g_up = draw_g_up(jax.random.fold_in(splits[8], 71), 0)
    g_down = draw_g_down(jax.random.fold_in(splits[8], 71), 0)
    cotangent = noise(splits[7], (TOKENS, D), 0.5, 6.0, ((0, 64), (1, 8)))
    return {"tokens": tokens, "w_gate": w_gate, "w_up": w_up, "w_down": w_down, "g_gate": g_gate, "g_up": g_up, "g_down": g_down, "cotangent": cotangent}


def gelu_product(gate_in, upper_in):
    return jax.nn.gelu(gate_in, approximate=True) * upper_in

def reference(tokens, w_gate, w_up, w_down, g_gate, g_up, g_down, cotangent):
    norm_sq = jnp.sum(jnp.square(g_gate.astype(jnp.float32)))
    norm_sq = norm_sq + jnp.sum(jnp.square(g_up.astype(jnp.float32)))
    norm_sq = norm_sq + jnp.sum(jnp.square(g_down.astype(jnp.float32)))
    step_scale = 0.7 * math.sqrt(3.0 * FF) / jnp.sqrt(norm_sq)
    pert_gate = (w_gate.astype(jnp.float32) + step_scale * g_gate.astype(jnp.float32)).astype(jnp.bfloat16)
    pert_up = (w_up.astype(jnp.float32) + step_scale * g_up.astype(jnp.float32)).astype(jnp.bfloat16)
    pert_down = (w_down.astype(jnp.float32) + step_scale * g_down.astype(jnp.float32)).astype(jnp.bfloat16)
    gate = jnp.dot(tokens, pert_gate, preferred_element_type=jnp.float32)
    upward = jnp.dot(tokens, pert_up, preferred_element_type=jnp.float32)
    hidden, pullback = jax.vjp(gelu_product, gate, upward)
    hidden = hidden.astype(jnp.bfloat16)
    d_hidden = jnp.dot(cotangent, pert_down.T, preferred_element_type=jnp.float32)
    d_gate, d_up = pullback(d_hidden)
    d_gate = d_gate.astype(jnp.bfloat16)
    d_up = d_up.astype(jnp.bfloat16)
    grad_gate = jnp.dot(tokens.T, d_gate, preferred_element_type=jnp.float32).astype(jnp.bfloat16)
    grad_up = jnp.dot(tokens.T, d_up, preferred_element_type=jnp.float32).astype(jnp.bfloat16)
    grad_down = jnp.dot(hidden.T, cotangent, preferred_element_type=jnp.float32).astype(jnp.bfloat16)
    grad_tokens = jnp.dot(d_gate, pert_gate.T, preferred_element_type=jnp.float32)
    grad_tokens = grad_tokens + jnp.dot(d_up, pert_up.T, preferred_element_type=jnp.float32)
    return (grad_tokens.astype(jnp.bfloat16), grad_gate, grad_up, grad_down)
```

```python
import functools
import math

import jax
import jax.numpy as jnp
from jax import lax
from jax.experimental import pallas as pl
from jax.experimental.pallas import tpu as pltpu
from jax.sharding import Mesh, PartitionSpec as P

FF = 24576
WIDTH = 576
UNITS = 384
ROWS = 64
PADDED = 640
bf16, f32 = jnp.bfloat16, jnp.float32
GELU_A = math.sqrt(2.0 / math.pi)
GELU_B = 0.044715
VMEM_BYTES = 40 * 1024 * 1024


def vmem_spec():
    return pl.BlockSpec(memory_space=pltpu.VMEM)


def smem_spec():
    return pl.BlockSpec(memory_space=pltpu.SMEM)


def kernel_call(kernel, outs, operands, flops, specs=None):
    size = sum(x.size * x.dtype.itemsize for x in list(operands) + list(outs))
    return pl.pallas_call(
        kernel,
        out_shape=outs,
        in_specs=specs or [vmem_spec()] * len(operands),
        out_specs=[vmem_spec()] * len(outs),
        compiler_params=pltpu.CompilerParams(vmem_limit_bytes=VMEM_BYTES),
        cost_estimate=pl.CostEstimate(flops=flops, bytes_accessed=size, transcendentals=0),
    )(*operands)


def shape(dims, dtype=bf16):
    return jax.ShapeDtypeStruct(dims, dtype)


def pack_kernel(tokens, cotangent, g_gate, g_up, g_down, out):
    total = jnp.zeros((16, UNITS), f32)
    for ref in (g_gate, g_up, g_down):
        for start in range(0, WIDTH, 16):
            part = ref[start : start + 16, :].astype(f32)
            total = total + part * part
    norm = jnp.sum(jnp.sum(total, axis=0, keepdims=True), axis=1, keepdims=True)
    high = norm.astype(bf16).astype(f32)
    middle = (norm - high).astype(bf16).astype(f32)
    low = norm - high - middle
    row = lax.broadcasted_iota(jnp.int32, (8, PADDED - WIDTH), 0)
    digits = jnp.where(row == 0, high, jnp.where(row == 1, middle, jnp.where(row == 2, low, 0.0)))
    out[:, 0:WIDTH] = tokens[...]
    out[:, WIDTH:PADDED] = digits.astype(bf16)
    out[:, PADDED : PADDED + WIDTH] = cotangent[...]
    out[:, PADDED + WIDTH :] = jnp.zeros((8, PADDED - WIDTH), bf16)


def dot(left, right, left_dim, right_dim):
    return lax.dot_general(
        left, right, (((left_dim,), (right_dim,)), ((), ())), preferred_element_type=f32
    )


def picked(chunks, core, low):
    return jnp.concatenate(
        [ref[pl.ds(pl.multiple_of(core * ROWS, ROWS), ROWS), low : low + WIDTH] for ref in chunks],
        axis=0,
    )


def forward_kernel(
    core_ref, scale_ref, c0, c1, c2, c3, w_gate, w_up, w_down, g_gate, g_up, g_down,
    send, keep, pert_gate, pert_up,
):
    core = core_ref[0]
    scale = scale_ref[0]
    chunks = (c0, c1, c2, c3)

    def perturbed(weight, saved):
        return (weight[...].astype(f32) + scale * saved[...].astype(f32)).astype(bf16)

    pert_gate[...] = perturbed(w_gate, g_gate)
    pert_up[...] = perturbed(w_up, g_up)
    pert_down = perturbed(w_down, g_down)
    for which, out in ((1 - core, send), (core, keep)):
        tokens = picked(chunks, which, 0)
        cotangent = picked(chunks, which, PADDED)
        out[:, 0:UNITS] = dot(tokens, pert_gate[...], 1, 0).astype(out.dtype)
        out[:, UNITS : 2 * UNITS] = dot(tokens, pert_up[...], 1, 0).astype(out.dtype)
        out[:, 2 * UNITS :] = dot(cotangent, pert_down, 1, 0).astype(out.dtype)


def hidden_kernel(parts, out):
    def total(which):
        low = which * UNITS
        acc = parts[0, :, low : low + UNITS].astype(f32)
        for k in range(1, 4):
            acc = acc + parts[k, :, low : low + UNITS].astype(f32)
        return acc

    gate, upward, d_hidden = total(0), total(1), total(2)
    square = gate * gate
    bend = jnp.tanh(GELU_A * (gate + GELU_B * (gate * square)))
    half = 0.5 * (1.0 + bend)
    active = gate * half
    slope = half + 0.5 * gate * (1.0 - bend * bend) * (GELU_A * (1.0 + 3.0 * GELU_B * square))
    out[:, 0:UNITS] = (active * upward).astype(bf16)
    out[:, UNITS : 2 * UNITS] = (d_hidden * upward * slope).astype(bf16)
    out[:, 2 * UNITS :] = (d_hidden * active).astype(bf16)


def tokens_kernel(core_ref, own, other, pert_gate, pert_up, out):
    core = core_ref[0]
    for which, ref in ((core, own), (1 - core, other)):
        value = dot(ref[:, UNITS : 2 * UNITS], pert_gate[...], 1, 1)
        value = value + dot(ref[:, 2 * UNITS :], pert_up[...], 1, 1)
        value = value.astype(bf16)
        for k in range(4):
            out[k, pl.ds(pl.multiple_of(which * ROWS, ROWS), ROWS), :] = value[
                k * ROWS : (k + 1) * ROWS
            ]


def weights_kernel(core_ref, c0, c1, c2, c3, own, other, grad_gate, grad_up, grad_down):
    core = core_ref[0]
    chunks = (c0, c1, c2, c3)
    hidden = jnp.concatenate([own[...], other[...]], axis=0)
    tokens = jnp.concatenate([picked(chunks, core, 0), picked(chunks, 1 - core, 0)], axis=0)
    cotangent = jnp.concatenate(
        [picked(chunks, core, PADDED), picked(chunks, 1 - core, PADDED)], axis=0
    )
    grad_gate[...] = dot(tokens, hidden[:, UNITS : 2 * UNITS], 0, 0).astype(bf16)
    grad_up[...] = dot(tokens, hidden[:, 2 * UNITS :], 0, 0).astype(bf16)
    grad_down[...] = dot(cotangent, hidden[:, 0:UNITS], 0, 0).astype(bf16)


def body(tokens, w_gate, w_up, w_down, g_gate, g_up, g_down, cotangent):
    w_down, g_down = w_down.T, g_down.T
    core = lax.axis_index("core").astype(jnp.int32).reshape(1)
    (packed,) = kernel_call(
        pack_kernel, [shape((8, 2 * PADDED))], (tokens, cotangent, g_gate, g_up, g_down), 2 * 3 * WIDTH * UNITS
    )
    mine = lax.all_gather(packed, "col", axis=0, tiled=True)
    norm = jnp.sum(mine[:, WIDTH].astype(f32))
    chunks = [mine] + [
        lax.ppermute(mine, "dp", [(i, (i - k) % 4) for i in range(4)]) for k in (1, 2, 3)
    ]
    norm_sq = lax.psum(lax.psum(norm, ("y", "core")), "dp")
    step_scale = (0.7 * math.sqrt(3.0 * FF) / jnp.sqrt(norm_sq)).reshape(1)
    mult = 512 * WIDTH * UNITS * 2
    operands = (core, step_scale, *chunks, w_gate, w_up, w_down, g_gate, g_up, g_down)
    send, keep, pert_gate, pert_up = kernel_call(
        forward_kernel,
        [shape((4 * ROWS, 3 * UNITS)), shape((4 * ROWS, 3 * UNITS), f32)] + [shape((WIDTH, UNITS))] * 2,
        operands,
        3 * mult,
        [smem_spec()] * 2 + [vmem_spec()] * 10,
    )
    swap = [(0, 1), (1, 0)]
    received = lax.ppermute(send, "core", swap)
    partial = (keep + received.astype(f32)).astype(bf16).reshape(4, ROWS, 3 * UNITS)
    parts = lax.all_to_all(partial, "y", 0, 0, tiled=True)
    (hidden,) = kernel_call(hidden_kernel, [shape((ROWS, 3 * UNITS))], (parts,), 30 * ROWS * UNITS)
    own = lax.all_gather(hidden, "y", axis=0, tiled=True)
    other = lax.ppermute(own, "core", swap)
    (grad_parts,) = kernel_call(
        tokens_kernel,
        [shape((4, 2 * ROWS, WIDTH))],
        (core, own, other, pert_gate, pert_up),
        2 * mult,
        [smem_spec()] + [vmem_spec()] * 4,
    )
    grad_gate, grad_up, grad_down = kernel_call(
        weights_kernel,
        [shape((WIDTH, UNITS))] * 3,
        (core, *chunks, own, other),
        3 * mult,
        [smem_spec()] + [vmem_spec()] * 6,
    )
    total = grad_parts[0].astype(f32)
    for k in (1, 2, 3):
        arrived = lax.ppermute(grad_parts[k], "dp", [(i, (i + k) % 4) for i in range(4)])
        total = total + arrived.astype(f32)
    pieces = lax.all_to_all(total.astype(bf16).reshape(16, 8, WIDTH), "col", 0, 0, tiled=True)
    grad_tokens = jnp.sum(pieces.astype(f32), axis=0).astype(bf16)
    return (grad_tokens, grad_gate, grad_up, grad_down.T)


def solution(mesh):
    fine = Mesh(mesh.devices.reshape(4, 4, 2, 16), ("dp", "y", "core", "col"))
    by_rows = P(("dp", "col"), ("y", "core"))
    by_columns = P(("y", "core"), ("dp", "col"))
    return jax.shard_map(
        body,
        mesh=fine,
        in_specs=(by_rows, by_columns, by_columns, by_rows, by_columns, by_columns, by_rows, by_rows),
        out_specs=(by_rows, by_columns, by_columns, by_rows),
        check_vma=False,
    )
```

```python
import math

import jax
import jax.numpy as jnp
from jax import lax
from jax.experimental import pallas as pl
from jax.experimental.pallas import tpu as pltpu
from jax.sharding import Mesh, PartitionSpec as P

FF = 24576
WIDTH = 576
UNITS = 384
ROWS = 64
PADDED = 640
bf16, f32 = jnp.bfloat16, jnp.float32
GELU_A = math.sqrt(2.0 / math.pi)
GELU_B = 0.044715
VMEM_BYTES = 24 * 1024 * 1024


def vmem_spec():
    return pl.BlockSpec(memory_space=pltpu.VMEM)


def smem_spec():
    return pl.BlockSpec(memory_space=pltpu.SMEM)


def kernel_call(kernel, outs, operands, flops, specs=None, grid=()):
    size = sum(x.size * x.dtype.itemsize for x in list(operands) + list(outs))
    return pl.pallas_call(
        kernel,
        grid=grid,
        out_shape=outs,
        in_specs=specs or [vmem_spec()] * len(operands),
        out_specs=[vmem_spec()] * len(outs),
        compiler_params=pltpu.CompilerParams(vmem_limit_bytes=VMEM_BYTES),
        cost_estimate=pl.CostEstimate(flops=flops, bytes_accessed=size, transcendentals=0),
    )(*operands)


def shape(dims, dtype=bf16):
    return jax.ShapeDtypeStruct(dims, dtype)


def whole_spec(x):
    return pl.BlockSpec(x.shape, lambda i: (0,) * len(x.shape))


def pack_kernel(tokens, cotangent, g_gate, g_up, g_down, out):
    total = jnp.zeros((16, UNITS), f32)
    for ref in (g_gate, g_up, g_down):
        for start in range(0, WIDTH, 16):
            part = ref[start : start + 16, :].astype(f32)
            total = total + part * part
    norm = jnp.sum(jnp.sum(total, axis=0, keepdims=True), axis=1, keepdims=True)
    high = norm.astype(bf16).astype(f32)
    middle = (norm - high).astype(bf16).astype(f32)
    low = norm - high - middle
    row = lax.broadcasted_iota(jnp.int32, (8, PADDED - WIDTH), 0)
    digits = jnp.where(row == 0, high, jnp.where(row == 1, middle, jnp.where(row == 2, low, 0.0)))
    out[:, 0:WIDTH] = tokens[...]
    out[:, WIDTH:PADDED] = digits.astype(bf16)
    out[:, PADDED : PADDED + WIDTH] = cotangent[...]
    out[:, PADDED + WIDTH :] = jnp.zeros((8, PADDED - WIDTH), bf16)


def spread_kernel(digits, out):
    block = digits[:, PADDED - 128 : PADDED].astype(f32)
    lane = lax.broadcasted_iota(jnp.int32, block.shape, 1)
    block = jnp.where(lane == 127, block, 0.0)
    total = jnp.sum(jnp.sum(block, axis=0, keepdims=True), axis=1, keepdims=True)
    out[...] = jnp.broadcast_to(total.reshape(1, 1, 1), out.shape)


def sum_kernel(parts, out):
    width = out.shape[1]
    total = parts[0, :, 0:width].astype(f32)
    for k in range(1, parts.shape[0]):
        total = total + parts[k, :, 0:width].astype(f32)
    out[...] = total.astype(bf16)


def dot(left, right, left_dim, right_dim):
    return lax.dot_general(
        left, right, (((left_dim,), (right_dim,)), ((), ())), preferred_element_type=f32
    )


def picked(chunks, core):
    return jnp.concatenate(
        [ref[pl.ds(pl.multiple_of(core * ROWS, ROWS), ROWS), :] for ref in chunks], axis=0
    )


def forward_kernel(
    place, norms, c0, c1, c2, c3, w_gate, w_up, w_down, g_gate, g_up, g_down,
    send, keep, pert_gate, pert_up, tokens_own, tokens_other,
):
    core = lax.rem(place[0], 2)
    norm_sq = jnp.sum(norms[...], axis=0)[0:1, 0:1]
    scale = 0.7 * math.sqrt(3.0 * FF) / jnp.sqrt(norm_sq)
    chunks = (c0, c1, c2, c3)

    def perturbed(weight, saved):
        return (weight[...].astype(f32) + scale * saved[...].astype(f32)).astype(bf16)

    pert_gate[...] = perturbed(w_gate, g_gate)
    pert_up[...] = perturbed(w_up, g_up)
    pert_down = perturbed(w_down, g_down)
    for which, out, rows in ((1 - core, send, tokens_other), (core, keep, tokens_own)):
        rows[...] = picked(chunks, which)
        tokens = rows[:, 0:WIDTH]
        cotangent = rows[:, PADDED : PADDED + WIDTH]
        out[:, 0:UNITS] = dot(tokens, pert_gate[...], 1, 0).astype(out.dtype)
        out[:, UNITS : 2 * UNITS] = dot(tokens, pert_up[...], 1, 0).astype(out.dtype)
        out[:, 2 * UNITS :] = dot(cotangent, pert_down, 1, 0).astype(out.dtype)


def hidden_kernel(parts, out):
    def total(which):
        low = which * UNITS
        acc = parts[0, :, low : low + UNITS].astype(f32)
        for k in range(1, 4):
            acc = acc + parts[k, :, low : low + UNITS].astype(f32)
        return acc

    gate, upward, d_hidden = total(0), total(1), total(2)
    square = gate * gate
    bend = jnp.tanh(GELU_A * (gate + GELU_B * (gate * square)))
    half = 0.5 * (1.0 + bend)
    active = gate * half
    slope = half + 0.5 * gate * (1.0 - bend * bend) * (GELU_A * (1.0 + 3.0 * GELU_B * square))
    out[:, 0:UNITS] = (active * upward).astype(bf16)
    out[:, UNITS : 2 * UNITS] = (d_hidden * upward * slope).astype(bf16)
    out[:, 2 * UNITS :] = (d_hidden * active).astype(bf16)


def tokens_kernel(place, own, other, pert_gate, pert_up, out):
    core = lax.rem(place[0], 2)
    for which, ref in ((core, own), (1 - core, other)):
        value = dot(ref[:, UNITS : 2 * UNITS], pert_gate[...], 1, 1)
        value = value + dot(ref[:, 2 * UNITS :], pert_up[...], 1, 1)
        value = jnp.pad(value.astype(bf16), ((0, 0), (0, PADDED - WIDTH)))
        for k in range(4):
            out[lax.rem(lax.div(place[0], 2) + k, 4), pl.ds(pl.multiple_of(which * ROWS, ROWS), ROWS), :] = value[
                k * ROWS : (k + 1) * ROWS
            ]


def weights_kernel(tokens_own, tokens_other, own, other, grad_gate, grad_up, grad_down):
    hidden = jnp.concatenate([own[...], other[...]], axis=0)
    rows = jnp.concatenate([tokens_own[...], tokens_other[...]], axis=0)
    tokens = rows[:, 0:WIDTH]
    cotangent = rows[:, PADDED : PADDED + WIDTH]
    grad_gate[...] = dot(tokens, hidden[:, UNITS : 2 * UNITS], 0, 0).astype(bf16)
    grad_up[...] = dot(tokens, hidden[:, 2 * UNITS :], 0, 0).astype(bf16)
    grad_down[...] = dot(cotangent, hidden[:, 0:UNITS], 0, 0).astype(bf16)


def body(tokens, w_gate, w_up, w_down, g_gate, g_up, g_down, cotangent):
    w_down, g_down = w_down.T, g_down.T
    place = (2 * lax.axis_index("dp") + lax.axis_index("core")).astype(jnp.int32).reshape(1)
    first = (tokens, cotangent, g_gate, g_up, g_down)
    packed = pl.pallas_call(
        pack_kernel,
        grid=(1,),
        out_shape=shape((8, 2 * PADDED)),
        in_specs=[whole_spec(x) for x in first],
        out_specs=vmem_spec(),
        compiler_params=pltpu.CompilerParams(vmem_limit_bytes=58 * 1024 * 1024),
        cost_estimate=pl.CostEstimate(flops=6 * WIDTH * UNITS, bytes_accessed=6 * WIDTH * UNITS, transcendentals=0),
    )(*first)
    mine = lax.all_gather(packed, "col", axis=0, tiled=True)
    chunks = [mine] + [
        lax.ppermute(mine, "dp", [(i, (i - k) % 4) for i in range(4)]) for k in (1, 2, 3)
    ]
    (norm,) = kernel_call(spread_kernel, [shape((32, 8, 128), f32)], (mine,), 128 * 128)
    norms = lax.all_to_all(norm, ("dp", "y", "core"), 0, 0, tiled=True)
    mult = 512 * WIDTH * UNITS * 2
    operands = (place, norms, *chunks, w_gate, w_up, w_down, g_gate, g_up, g_down)
    send, keep, pert_gate, pert_up, tokens_own, tokens_other = kernel_call(
        forward_kernel,
        [shape((4 * ROWS, 3 * UNITS)), shape((4 * ROWS, 3 * UNITS), f32)] + [shape((WIDTH, UNITS))] * 2 + [shape((4 * ROWS, 2 * PADDED))] * 2,
        operands,
        3 * mult,
        [smem_spec()] + [vmem_spec()] * 11,
    )
    swap = [(0, 1), (1, 0)]
    received = lax.ppermute(send, "core", swap)
    partial = (keep + received.astype(f32)).astype(bf16).reshape(4, ROWS, 3 * UNITS)
    parts = lax.all_to_all(partial, "y", 0, 0, tiled=True)
    (hidden,) = kernel_call(hidden_kernel, [shape((ROWS, 3 * UNITS))], (parts,), 30 * ROWS * UNITS)
    own = lax.all_gather(hidden, "y", axis=0, tiled=True)
    other = lax.ppermute(own, "core", swap)
    (grad_parts,) = kernel_call(
        tokens_kernel,
        [shape((4, 2 * ROWS, PADDED))],
        (place, own, other, pert_gate, pert_up),
        2 * mult,
        [smem_spec()] + [vmem_spec()] * 4,
    )
    grad_gate, grad_up, grad_down = kernel_call(
        weights_kernel,
        [shape((WIDTH, UNITS))] * 3,
        (tokens_own, tokens_other, own, other),
        3 * mult,
    )
    arrived = lax.all_to_all(grad_parts, "dp", 0, 0, tiled=True)
    (line,) = kernel_call(sum_kernel, [shape((2 * ROWS, WIDTH))], (arrived,), 4 * 128 * WIDTH)
    pieces = lax.all_to_all(line.reshape(16, 8, WIDTH), "col", 0, 0, tiled=True)
    (grad_tokens,) = kernel_call(sum_kernel, [shape((8, WIDTH))], (pieces,), 128 * WIDTH)
    return (grad_tokens, grad_gate, grad_up, grad_down.T)


def solution(mesh):
    fine = Mesh(mesh.devices.reshape(4, 4, 2, 16), ("dp", "y", "core", "col"))
    by_rows = P(("dp", "col"), ("y", "core"))
    by_columns = P(("y", "core"), ("dp", "col"))
    return jax.shard_map(
        body,
        mesh=fine,
        in_specs=(by_rows, by_columns, by_columns, by_rows, by_columns, by_columns, by_rows, by_rows),
        out_specs=(by_rows, by_columns, by_columns, by_rows),
        check_vma=False,
    )
```

```python
import functools
import math

import jax
import jax.numpy as jnp
from jax import lax
from jax.experimental import pallas as pl
from jax.experimental.pallas import tpu as pltpu
from jax.sharding import Mesh, PartitionSpec as P

FF = 24576
WIDTH = 576
UNITS = 384
ROWS = 64
PADDED = 640
bf16, f32 = jnp.bfloat16, jnp.float32
GELU_A = math.sqrt(2.0 / math.pi)
GELU_B = 0.044715
VMEM_BYTES = 16 * 1024 * 1024


def vmem_spec():
    return pl.BlockSpec(memory_space=pltpu.VMEM)


def smem_spec():
    return pl.BlockSpec(memory_space=pltpu.SMEM)


def kernel_call(kernel, outs, operands, flops, specs=None, grid=(), aliases=None):
    size = sum(x.size * x.dtype.itemsize for x in list(operands) + list(outs))
    return pl.pallas_call(
        kernel,
        grid=grid,
        out_shape=outs,
        input_output_aliases=aliases or {},
        in_specs=specs or [vmem_spec()] * len(operands),
        out_specs=[vmem_spec()] * len(outs),
        compiler_params=pltpu.CompilerParams(vmem_limit_bytes=VMEM_BYTES),
        cost_estimate=pl.CostEstimate(flops=flops, bytes_accessed=size, transcendentals=0),
    )(*operands)


def shape(dims, dtype=bf16):
    return jax.ShapeDtypeStruct(dims, dtype)


def whole_spec(x):
    return pl.BlockSpec(x.shape, lambda i: (0,) * len(x.shape))


def pack_kernel(tokens, cotangent, g_gate, g_up, g_down, out):
    total = jnp.zeros((16, UNITS), f32)
    for ref in (g_gate, g_up, g_down):
        for start in range(0, WIDTH, 16):
            part = ref[start : start + 16, :].astype(f32)
            total = total + part * part
    norm = jnp.sum(jnp.sum(total, axis=0, keepdims=True), axis=1, keepdims=True)
    high = norm.astype(bf16).astype(f32)
    middle = (norm - high).astype(bf16).astype(f32)
    low = norm - high - middle
    row = lax.broadcasted_iota(jnp.int32, (8, PADDED - WIDTH), 0)
    digits = jnp.where(row == 0, high, jnp.where(row == 1, middle, jnp.where(row == 2, low, 0.0)))
    out[:, 0:WIDTH] = tokens[...]
    out[:, WIDTH:PADDED] = digits.astype(bf16)
    out[:, PADDED : PADDED + WIDTH] = cotangent[...]
    out[:, PADDED + WIDTH :] = jnp.zeros((8, PADDED - WIDTH), bf16)


def spread_kernel(digits, out):
    block = digits[:, PADDED - 128 : PADDED].astype(f32)
    lane = lax.broadcasted_iota(jnp.int32, block.shape, 1)
    block = jnp.where(lane == 127, block, 0.0)
    total = jnp.sum(jnp.sum(block, axis=0, keepdims=True), axis=1, keepdims=True)
    out[...] = jnp.broadcast_to(total.reshape(1, 1, 1), out.shape)


def sum_kernel(parts, out):
    width = out.shape[1]
    total = parts[0, :, 0:width].astype(f32)
    for k in range(1, parts.shape[0]):
        total = total + parts[k, :, 0:width].astype(f32)
    out[...] = total.astype(bf16)


def dot(left, right, left_dim, right_dim):
    return lax.dot_general(
        left, right, (((left_dim,), (right_dim,)), ((), ())), preferred_element_type=f32
    )


def picked(chunks, core):
    return jnp.concatenate(
        [ref[pl.ds(pl.multiple_of(core * ROWS, ROWS), ROWS), :] for ref in chunks], axis=0
    )


def load_kernel(after, w_gate, w_up, w_down, g_gate, g_up, g_down, held):
    del after
    for k, ref in enumerate((w_gate, w_up, w_down, g_gate, g_up, g_down)):
        held[k] = ref[...]


def perturb_kernel(norms, held, p_gate, p_up, p_down):
    norm_sq = jnp.sum(norms[...], axis=0)[0:1, 0:1]
    scale = 0.7 * math.sqrt(3.0 * FF) / jnp.sqrt(norm_sq)
    for k, out in enumerate((p_gate, p_up, p_down)):
        out[...] = (held[k].astype(f32) + scale * held[3 + k].astype(f32)).astype(bf16)


def forward_kernel(flip, place, c0, c1, c2, c3, p_gate, p_up, p_down, out, rows):
    core = lax.rem(place[0], 2)
    rows[...] = picked((c0, c1, c2, c3), 1 - core if flip else core)
    tokens = rows[:, 0:WIDTH]
    cotangent = rows[:, PADDED : PADDED + WIDTH]
    out[:, 0:UNITS] = dot(tokens, p_gate[...], 1, 0).astype(out.dtype)
    out[:, UNITS : 2 * UNITS] = dot(tokens, p_up[...], 1, 0).astype(out.dtype)
    out[:, 2 * UNITS :] = dot(cotangent, p_down[...], 1, 0).astype(out.dtype)


def hidden_kernel(parts, out):
    def total(which):
        low = which * UNITS
        acc = parts[0, :, low : low + UNITS].astype(f32)
        for k in range(1, 4):
            acc = acc + parts[k, :, low : low + UNITS].astype(f32)
        return acc

    gate, upward, d_hidden = total(0), total(1), total(2)
    square = gate * gate
    bend = jnp.tanh(GELU_A * (gate + GELU_B * (gate * square)))
    half = 0.5 * (1.0 + bend)
    active = gate * half
    slope = half + 0.5 * gate * (1.0 - bend * bend) * (GELU_A * (1.0 + 3.0 * GELU_B * square))
    out[:, 0:UNITS] = (active * upward).astype(bf16)
    out[:, UNITS : 2 * UNITS] = (d_hidden * upward * slope).astype(bf16)
    out[:, 2 * UNITS :] = (d_hidden * active).astype(bf16)


def tokens_kernel(flip, place, rows, p_gate, p_up, *rest):
    out = rest[-1]
    core = lax.rem(place[0], 2)
    half = 1 - core if flip else core
    value = dot(rows[:, UNITS : 2 * UNITS], p_gate[...], 1, 1)
    value = value + dot(rows[:, 2 * UNITS :], p_up[...], 1, 1)
    value = jnp.pad(value.astype(bf16), ((0, 0), (0, PADDED - WIDTH)))
    for k in range(4):
        out[lax.rem(lax.div(place[0], 2) + k, 4), pl.ds(pl.multiple_of(half * ROWS, ROWS), ROWS), :] = value[
            k * ROWS : (k + 1) * ROWS
        ]


def weights_kernel(tokens_own, tokens_other, own, other, grad_gate, grad_up, grad_down):
    hidden = jnp.concatenate([own[...], other[...]], axis=0)
    rows = jnp.concatenate([tokens_own[...], tokens_other[...]], axis=0)
    tokens = rows[:, 0:WIDTH]
    cotangent = rows[:, PADDED : PADDED + WIDTH]
    grad_gate[...] = dot(tokens, hidden[:, UNITS : 2 * UNITS], 0, 0).astype(bf16)
    grad_up[...] = dot(tokens, hidden[:, 2 * UNITS :], 0, 0).astype(bf16)
    grad_down[...] = dot(cotangent, hidden[:, 0:UNITS], 0, 0).astype(bf16)


def body(tokens, w_gate, w_up, w_down, g_gate, g_up, g_down, cotangent):
    w_down, g_down = w_down.T, g_down.T
    place = (2 * lax.axis_index("dp") + lax.axis_index("core")).astype(jnp.int32).reshape(1)
    first = (tokens, cotangent, g_gate, g_up, g_down)
    packed = pl.pallas_call(
        pack_kernel,
        grid=(1,),
        out_shape=shape((8, 2 * PADDED)),
        in_specs=[whole_spec(x) for x in first],
        out_specs=vmem_spec(),
        compiler_params=pltpu.CompilerParams(vmem_limit_bytes=58 * 1024 * 1024),
        cost_estimate=pl.CostEstimate(flops=6 * WIDTH * UNITS, bytes_accessed=6 * WIDTH * UNITS, transcendentals=0),
    )(*first)
    mine = lax.all_gather(packed, "col", axis=0, tiled=True)
    chunks = [mine] + [
        lax.ppermute(mine, "dp", [(i, (i - k) % 4) for i in range(4)]) for k in (1, 2, 3)
    ]
    (norm,) = kernel_call(spread_kernel, [shape((32, 8, 128), f32)], (mine,), 128 * 128)
    norms = lax.all_to_all(norm, ("dp", "y", "core"), 0, 0, tiled=True)
    mult = 512 * WIDTH * UNITS * 2
    loaded = (norm, w_gate, w_up, w_down, g_gate, g_up, g_down)
    (held,) = kernel_call(
        load_kernel,
        [shape((6, WIDTH, UNITS))],
        loaded,
        0,
        [pl.BlockSpec(memory_space=pl.ANY)] + [whole_spec(x) for x in loaded[1:]],
        (1,),
    )
    perturbed = kernel_call(
        perturb_kernel,
        [shape((WIDTH, UNITS))] * 3,
        (norms, held),
        6 * WIDTH * UNITS,
    )
    half = [shape((4 * ROWS, 3 * UNITS)), shape((4 * ROWS, 2 * PADDED))]
    send, tokens_other = kernel_call(
        functools.partial(forward_kernel, True),
        half,
        (place, *chunks, *perturbed),
        3 * mult // 2,
        [smem_spec()] + [vmem_spec()] * 7,
    )
    half[0] = shape((4 * ROWS, 3 * UNITS), f32)
    keep, tokens_own = kernel_call(
        functools.partial(forward_kernel, False),
        half,
        (place, *chunks, *perturbed),
        3 * mult // 2,
        [smem_spec()] + [vmem_spec()] * 7,
    )
    swap = [(0, 1), (1, 0)]
    received = lax.ppermute(send, "core", swap)
    partial = (keep + received.astype(f32)).astype(bf16).reshape(4, ROWS, 3 * UNITS)
    parts = lax.all_to_all(partial, "y", 0, 0, tiled=True)
    (hidden,) = kernel_call(hidden_kernel, [shape((ROWS, 3 * UNITS))], (parts,), 30 * ROWS * UNITS)
    own = lax.all_gather(hidden, "y", axis=0, tiled=True)
    other = lax.ppermute(own, "core", swap)
    (grad_parts,) = kernel_call(
        functools.partial(tokens_kernel, False),
        [shape((4, 2 * ROWS, PADDED))],
        (place, own, perturbed[0], perturbed[1]),
        mult,
        [smem_spec()] + [vmem_spec()] * 3,
    )
    (grad_parts,) = kernel_call(
        functools.partial(tokens_kernel, True),
        [shape((4, 2 * ROWS, PADDED))],
        (place, other, perturbed[0], perturbed[1], grad_parts),
        mult,
        [smem_spec()] + [vmem_spec()] * 3 + [pl.BlockSpec(memory_space=pl.ANY)],
        aliases={4: 0},
    )
    grad_gate, grad_up, grad_down = kernel_call(
        weights_kernel,
        [shape((WIDTH, UNITS))] * 3,
        (tokens_own, tokens_other, own, other),
        3 * mult,
    )
    arrived = lax.all_to_all(grad_parts, "dp", 0, 0, tiled=True)
    (line,) = kernel_call(sum_kernel, [shape((2 * ROWS, WIDTH))], (arrived,), 4 * 128 * WIDTH)
    pieces = lax.all_to_all(line.reshape(16, 8, WIDTH), "col", 0, 0, tiled=True)
    (grad_tokens,) = kernel_call(sum_kernel, [shape((8, WIDTH))], (pieces,), 128 * WIDTH)
    return (grad_tokens, grad_gate, grad_up, grad_down.T)


def solution(mesh):
    fine = Mesh(mesh.devices.reshape(4, 4, 2, 16), ("dp", "y", "core", "col"))
    by_rows = P(("dp", "col"), ("y", "core"))
    by_columns = P(("y", "core"), ("dp", "col"))
    return jax.shard_map(
        body,
        mesh=fine,
        in_specs=(by_rows, by_columns, by_columns, by_rows, by_columns, by_columns, by_rows, by_rows),
        out_specs=(by_rows, by_columns, by_columns, by_rows),
        check_vma=False,
    )
```

```python
import functools
import math

import jax
import jax.numpy as jnp
from jax import lax
from jax.experimental import pallas as pl
from jax.experimental.pallas import tpu as pltpu
from jax.sharding import Mesh, PartitionSpec as P

FF = 24576
WIDTH = 576
UNITS = 384
ROWS = 64
PADDED = 640
bf16, f32 = jnp.bfloat16, jnp.float32
GELU_A = math.sqrt(2.0 / math.pi)
GELU_B = 0.044715
VMEM_BYTES = 16 * 1024 * 1024


def vmem_spec():
    return pl.BlockSpec(memory_space=pltpu.VMEM)


def smem_spec():
    return pl.BlockSpec(memory_space=pltpu.SMEM)


def kernel_call(kernel, outs, operands, flops, specs=None, grid=(), aliases=None, scratch=()):
    size = sum(x.size * x.dtype.itemsize for x in list(operands) + list(outs))
    return pl.pallas_call(
        kernel,
        grid=grid,
        out_shape=outs,
        scratch_shapes=scratch,
        input_output_aliases=aliases or {},
        in_specs=specs or [vmem_spec()] * len(operands),
        out_specs=[vmem_spec()] * len(outs),
        compiler_params=pltpu.CompilerParams(vmem_limit_bytes=VMEM_BYTES),
        cost_estimate=pl.CostEstimate(flops=flops, bytes_accessed=size, transcendentals=0),
    )(*operands)


def shape(dims, dtype=bf16):
    return jax.ShapeDtypeStruct(dims, dtype)


def whole_spec(x):
    return pl.BlockSpec(x.shape, lambda i: (0,) * len(x.shape))


def pack_kernel(tokens, cotangent, g_gate, g_up, g_down, out):
    total = jnp.zeros((16, UNITS), f32)
    for ref in (g_gate, g_up, g_down):
        for start in range(0, WIDTH, 16):
            part = ref[start : start + 16, :].astype(f32)
            total = total + part * part
    norm = jnp.sum(jnp.sum(total, axis=0, keepdims=True), axis=1, keepdims=True)
    high = norm.astype(bf16).astype(f32)
    middle = (norm - high).astype(bf16).astype(f32)
    low = norm - high - middle
    row = lax.broadcasted_iota(jnp.int32, (8, PADDED - WIDTH), 0)
    digits = jnp.where(row == 0, high, jnp.where(row == 1, middle, jnp.where(row == 2, low, 0.0)))
    out[:, 0:WIDTH] = tokens[...]
    out[:, WIDTH:PADDED] = digits.astype(bf16)
    out[:, PADDED : PADDED + WIDTH] = cotangent[...]
    out[:, PADDED + WIDTH :] = jnp.zeros((8, PADDED - WIDTH), bf16)


def spread_kernel(digits, out):
    block = digits[:, PADDED - 128 : PADDED].astype(f32)
    lane = lax.broadcasted_iota(jnp.int32, block.shape, 1)
    block = jnp.where(lane == 127, block, 0.0)
    total = jnp.sum(jnp.sum(block, axis=0, keepdims=True), axis=1, keepdims=True)
    out[...] = jnp.broadcast_to(total.reshape(1, 1, 1), out.shape)


def sum_kernel(parts, out):
    width = out.shape[1]
    total = parts[0, :, 0:width].astype(f32)
    for k in range(1, parts.shape[0]):
        total = total + parts[k, :, 0:width].astype(f32)
    out[...] = total.astype(bf16)


def dot(left, right, left_dim, right_dim):
    return lax.dot_general(
        left, right, (((left_dim,), (right_dim,)), ((), ())), preferred_element_type=f32
    )


def load_kernel(after, w_gate, w_up, w_down, g_gate, g_up, g_down, held):
    del after
    for k, ref in enumerate((w_gate, w_up, w_down, g_gate, g_up, g_down)):
        held[k] = ref[...]


def fetched(half, chunks, rows, done, base=0):
    start = pl.multiple_of(half * ROWS, ROWS)
    copies = []
    for k, chunk in enumerate(chunks):
        source = chunk.at[pl.ds(start, ROWS), :]
        target = rows.at[pl.ds((base + k) * ROWS, ROWS), :]
        copies.append(pltpu.make_async_copy(source, target, done.at[base + k]))
    for copy in copies:
        copy.start()
    return copies


def products(rows, p_gate, p_up, p_down, out):
    tokens = rows[:, 0:WIDTH]
    cotangent = rows[:, PADDED : PADDED + WIDTH]
    out[:, 0:UNITS] = dot(tokens, p_gate[...], 1, 0).astype(out.dtype)
    out[:, UNITS : 2 * UNITS] = dot(tokens, p_up[...], 1, 0).astype(out.dtype)
    out[:, 2 * UNITS :] = dot(cotangent, p_down[...], 1, 0).astype(out.dtype)


def send_kernel(place, norms, held, c0, c1, c2, c3, out, p_gate, p_up, p_down, rows, done):
    copies = fetched(1 - lax.rem(place[0], 2), (c0, c1, c2, c3), rows, done)
    norm_sq = jnp.sum(norms[...], axis=0)[0:1, 0:1]
    scale = 0.7 * math.sqrt(3.0 * FF) / jnp.sqrt(norm_sq)
    for k, pert in enumerate((p_gate, p_up, p_down)):
        pert[...] = (held[k].astype(f32) + scale * held[3 + k].astype(f32)).astype(bf16)
    for copy in copies:
        copy.wait()
    products(rows, p_gate, p_up, p_down, out)


def keep_kernel(place, c0, c1, c2, c3, p_gate, p_up, p_down, out, rows, done):
    for copy in fetched(lax.rem(place[0], 2), (c0, c1, c2, c3), rows, done):
        copy.wait()
    products(rows, p_gate, p_up, p_down, out)


def hidden_kernel(parts, copies, hidden):
    def total(which):
        low = which * UNITS
        acc = parts[0, :, low : low + UNITS].astype(f32)
        for k in range(1, 4):
            acc = acc + parts[k, :, low : low + UNITS].astype(f32)
        return acc

    gate, upward, d_hidden = total(0), total(1), total(2)
    square = gate * gate
    bend = jnp.tanh(GELU_A * (gate + GELU_B * (gate * square)))
    half = 0.5 * (1.0 + bend)
    active = gate * half
    slope = half + 0.5 * gate * (1.0 - bend * bend) * (GELU_A * (1.0 + 3.0 * GELU_B * square))
    hidden[...] = (active * upward).astype(bf16)
    d_gate = (d_hidden * upward * slope).astype(bf16)
    d_up = (d_hidden * active).astype(bf16)
    for k in range(4):
        copies[k, :, 0:UNITS] = d_gate
        copies[k, :, UNITS:] = d_up


def tokens_kernel(flip, place, rows, p_gate, p_up, *rest):
    out = rest[-1]
    core = lax.rem(place[0], 2)
    half = 1 - core if flip else core
    value = dot(rows[:, 0:UNITS], p_gate[...], 1, 1)
    value = value + dot(rows[:, UNITS:], p_up[...], 1, 1)
    value = jnp.pad(value.astype(bf16), ((0, 0), (0, PADDED - WIDTH)))
    for k in range(4):
        out[lax.rem(lax.div(place[0], 8) + k, 4), pl.ds(pl.multiple_of(half * ROWS, ROWS), ROWS), :] = value[
            k * ROWS : (k + 1) * ROWS
        ]


def weights_kernel(place, c0, c1, c2, c3, own, other, grad_gate, grad_up, rows, done):
    copies = []
    for k, chunk in enumerate((c0, c1, c2, c3)):
        target = rows.at[pl.ds(2 * k * ROWS, 2 * ROWS), :]
        copies.append(pltpu.make_async_copy(chunk, target, done.at[k]))
    for copy in copies:
        copy.start()
    for copy in copies:
        copy.wait()
    core = lax.rem(place[0], 2)
    tokens = []
    for half in (core, 1 - core):
        for k in range(4):
            start = pl.multiple_of(2 * k * ROWS + half * ROWS, ROWS)
            tokens.append(rows[pl.ds(start, ROWS), 0:WIDTH])
    tokens = jnp.concatenate(tokens, axis=0)
    moved = jnp.concatenate([own[...], other[...]], axis=0)
    grad_gate[...] = dot(tokens, moved[:, 0:UNITS], 0, 0).astype(bf16)
    grad_up[...] = dot(tokens, moved[:, UNITS:], 0, 0).astype(bf16)


def down_kernel(place, rows, h0, h1, h2, h3, grad_down):
    y = lax.div(lax.rem(place[0], 8), 2)
    cotangent = []
    for k in range(4):
        start = pl.multiple_of(lax.rem(y + k, 4) * 2 * ROWS, 2 * ROWS)
        cotangent.append(rows[pl.ds(start, 2 * ROWS), PADDED : PADDED + WIDTH])
    cotangent = jnp.concatenate(cotangent, axis=0)
    hidden = jnp.concatenate([h0[...], h1[...], h2[...], h3[...]], axis=0)
    grad_down[...] = dot(cotangent, hidden, 0, 0).astype(bf16)


def body(tokens, w_gate, w_up, w_down, g_gate, g_up, g_down, cotangent):
    w_down, g_down = w_down.T, g_down.T
    place = 8 * lax.axis_index("dp") + 2 * lax.axis_index("y") + lax.axis_index("core")
    place = place.astype(jnp.int32).reshape(1)
    first = (tokens, cotangent, g_gate, g_up, g_down)
    packed = pl.pallas_call(
        pack_kernel,
        grid=(1,),
        out_shape=shape((8, 2 * PADDED)),
        in_specs=[whole_spec(x) for x in first],
        out_specs=vmem_spec(),
        compiler_params=pltpu.CompilerParams(vmem_limit_bytes=58 * 1024 * 1024),
        cost_estimate=pl.CostEstimate(flops=6 * WIDTH * UNITS, bytes_accessed=6 * WIDTH * UNITS, transcendentals=0),
    )(*first)
    mine = lax.all_gather(packed, "col", axis=0, tiled=True)
    chunks = [mine] + [
        lax.ppermute(mine, "dp", [(i, (i - k) % 4) for i in range(4)]) for k in (1, 2, 3)
    ]
    (norm,) = kernel_call(spread_kernel, [shape((32, 8, 128), f32)], (mine,), 128 * 128)
    norms = lax.all_to_all(norm, ("dp", "y", "core"), 0, 0, tiled=True)
    mult = 512 * WIDTH * UNITS * 2
    loaded = (norm, w_gate, w_up, w_down, g_gate, g_up, g_down)
    (held,) = kernel_call(
        load_kernel,
        [shape((6, WIDTH, UNITS))],
        loaded,
        0,
        [pl.BlockSpec(memory_space=pl.ANY)] + [whole_spec(x) for x in loaded[1:]],
        (1,),
    )
    anywhere = [pl.BlockSpec(memory_space=pl.ANY)] * 4
    fetch = [pltpu.VMEM((4 * ROWS, 2 * PADDED), bf16), pltpu.SemaphoreType.DMA((4,))]
    send, *perturbed = kernel_call(
        send_kernel,
        [shape((4 * ROWS, 3 * UNITS))] + [shape((WIDTH, UNITS))] * 3,
        (place, norms, held, *chunks),
        3 * mult // 2,
        [smem_spec()] + [vmem_spec()] * 2 + anywhere,
        scratch=fetch,
    )
    (keep,) = kernel_call(
        keep_kernel,
        [shape((4 * ROWS, 3 * UNITS), f32)],
        (place, *chunks, *perturbed),
        3 * mult // 2,
        [smem_spec()] + anywhere + [vmem_spec()] * 3,
        scratch=fetch,
    )
    swap = [(0, 1), (1, 0)]
    received = lax.ppermute(send, "core", swap)
    partial = (keep + received.astype(f32)).astype(bf16).reshape(4, ROWS, 3 * UNITS)
    parts = lax.all_to_all(partial, "y", 0, 0, tiled=True)
    moved, hidden = kernel_call(
        hidden_kernel,
        [shape((4, ROWS, 2 * UNITS)), shape((ROWS, UNITS))],
        (parts,),
        30 * ROWS * UNITS,
    )
    own = lax.all_to_all(moved, "y", 0, 0, tiled=True).reshape(4 * ROWS, 2 * UNITS)
    other = lax.ppermute(own, "core", swap)
    (grad_parts,) = kernel_call(
        functools.partial(tokens_kernel, False),
        [shape((4, 2 * ROWS, PADDED))],
        (place, own, perturbed[0], perturbed[1]),
        mult,
        [smem_spec()] + [vmem_spec()] * 3,
    )
    (grad_parts,) = kernel_call(
        functools.partial(tokens_kernel, True),
        [shape((4, 2 * ROWS, PADDED))],
        (place, other, perturbed[0], perturbed[1], grad_parts),
        mult,
        [smem_spec()] + [vmem_spec()] * 3 + [pl.BlockSpec(memory_space=pl.ANY)],
        aliases={4: 0},
    )
    arrived = lax.all_to_all(grad_parts, "dp", 0, 0, tiled=True)
    (line,) = kernel_call(sum_kernel, [shape((2 * ROWS, WIDTH))], (arrived,), 4 * 128 * WIDTH)
    line, hidden = lax.optimization_barrier((line, hidden))
    pieces = lax.all_to_all(line.reshape(16, 8, WIDTH), "col", 0, 0, tiled=True)
    pair = lax.all_gather(hidden, "core", axis=0, tiled=True)
    pairs = [pair] + [
        lax.ppermute(pair, "y", [(i, (i - k) % 4) for i in range(4)]) for k in (1, 2, 3)
    ]
    grad_gate, grad_up, rows = kernel_call(
        weights_kernel,
        [shape((WIDTH, UNITS))] * 2 + [shape((8 * ROWS, 2 * PADDED))],
        (place, *chunks, own, other),
        2 * mult,
        [smem_spec()] + anywhere + [vmem_spec()] * 2,
        scratch=[pltpu.SemaphoreType.DMA((4,))],
    )
    (grad_down,) = kernel_call(
        down_kernel,
        [shape((WIDTH, UNITS))],
        (place, rows, *pairs),
        mult,
        [smem_spec()] + [vmem_spec()] * 5,
    )
    (grad_tokens,) = kernel_call(sum_kernel, [shape((8, WIDTH))], (pieces,), 128 * WIDTH)
    return (grad_tokens, grad_gate, grad_up, grad_down.T)


def solution(mesh):
    fine = Mesh(mesh.devices.reshape(4, 4, 2, 16), ("dp", "y", "core", "col"))
    by_rows = P(("dp", "col"), ("y", "core"))
    by_columns = P(("y", "core"), ("dp", "col"))
    return jax.shard_map(
        body,
        mesh=fine,
        in_specs=(by_rows, by_columns, by_columns, by_rows, by_columns, by_columns, by_rows, by_rows),
        out_specs=(by_rows, by_columns, by_columns, by_rows),
        check_vma=False,
    )
```

```python
import functools
import math

import jax
import jax.numpy as jnp
from jax import lax
from jax.experimental import pallas as pl
from jax.experimental.pallas import tpu as pltpu
from jax.sharding import Mesh, PartitionSpec as P

FF = 24576
WIDTH = 576
UNITS = 384
ROWS = 64
PADDED = 640
bf16, f32 = jnp.bfloat16, jnp.float32
GELU_A = math.sqrt(2.0 / math.pi)
GELU_B = 0.044715
VMEM_BYTES = 16 * 1024 * 1024


def vmem_spec():
    return pl.BlockSpec(memory_space=pltpu.VMEM)


def smem_spec():
    return pl.BlockSpec(memory_space=pltpu.SMEM)


def kernel_call(kernel, outs, operands, flops, specs=None, grid=(), aliases=None, scratch=()):
    size = sum(x.size * x.dtype.itemsize for x in list(operands) + list(outs))
    return pl.pallas_call(
        kernel,
        grid=grid,
        out_shape=outs,
        scratch_shapes=scratch,
        input_output_aliases=aliases or {},
        in_specs=specs or [vmem_spec()] * len(operands),
        out_specs=[vmem_spec()] * len(outs),
        compiler_params=pltpu.CompilerParams(vmem_limit_bytes=VMEM_BYTES),
        cost_estimate=pl.CostEstimate(flops=flops, bytes_accessed=size, transcendentals=0),
    )(*operands)


def shape(dims, dtype=bf16):
    return jax.ShapeDtypeStruct(dims, dtype)


def whole_spec(x):
    return pl.BlockSpec(x.shape, lambda i: (0,) * len(x.shape))


def pack_kernel(tokens, cotangent, g_gate, g_up, g_down, out):
    total = jnp.zeros((16, UNITS), f32)
    for ref in (g_gate, g_up, g_down):
        for start in range(0, WIDTH, 16):
            part = ref[start : start + 16, :].astype(f32)
            total = total + part * part
    norm = jnp.sum(jnp.sum(total, axis=0, keepdims=True), axis=1, keepdims=True)
    high = norm.astype(bf16).astype(f32)
    middle = (norm - high).astype(bf16).astype(f32)
    low = norm - high - middle
    row = lax.broadcasted_iota(jnp.int32, (8, PADDED - WIDTH), 0)
    digits = jnp.where(row == 0, high, jnp.where(row == 1, middle, jnp.where(row == 2, low, 0.0)))
    out[:, 0:WIDTH] = tokens[...]
    out[:, WIDTH:PADDED] = digits.astype(bf16)
    out[:, PADDED : PADDED + WIDTH] = cotangent[...]
    out[:, PADDED + WIDTH :] = jnp.zeros((8, PADDED - WIDTH), bf16)


def spread_kernel(digits, out):
    block = digits[:, PADDED - 128 : PADDED].astype(f32)
    lane = lax.broadcasted_iota(jnp.int32, block.shape, 1)
    block = jnp.where(lane == 127, block, 0.0)
    total = jnp.sum(jnp.sum(block, axis=0, keepdims=True), axis=1, keepdims=True)
    out[...] = jnp.broadcast_to(total.reshape(1, 1, 1), out.shape)


def line_kernel(parts, out):
    total = parts[0].astype(f32)
    for k in range(1, 4):
        total = total + parts[k].astype(f32)
    out[0:ROWS, :] = total[:, 0:WIDTH].astype(bf16)
    out[ROWS:, :] = total[:, WIDTH:].astype(bf16)


def sum_kernel(parts, out):
    width = out.shape[1]
    total = parts[0, :, 0:width].astype(f32)
    for k in range(1, parts.shape[0]):
        total = total + parts[k, :, 0:width].astype(f32)
    out[...] = total.astype(bf16)


def dot(left, right, left_dim, right_dim):
    return lax.dot_general(
        left, right, (((left_dim,), (right_dim,)), ((), ())), preferred_element_type=f32
    )


def load_kernel(after, w_gate, w_up, w_down, g_gate, g_up, g_down, held):
    del after
    for k, ref in enumerate((w_gate, w_up, w_down, g_gate, g_up, g_down)):
        held[k] = ref[...]


def fetched(half, chunks, rows, done, base=0):
    start = pl.multiple_of(half * ROWS, ROWS)
    copies = []
    for k, chunk in enumerate(chunks):
        source = chunk.at[pl.ds(start, ROWS), :]
        target = rows.at[pl.ds((base + k) * ROWS, ROWS), :]
        copies.append(pltpu.make_async_copy(source, target, done.at[base + k]))
    for copy in copies:
        copy.start()
    return copies


def products(rows, p_gate, p_up, p_down, out):
    tokens = rows[:, 0:WIDTH]
    cotangent = rows[:, PADDED : PADDED + WIDTH]
    out[:, 0:UNITS] = dot(tokens, p_gate[...], 1, 0).astype(out.dtype)
    out[:, UNITS : 2 * UNITS] = dot(tokens, p_up[...], 1, 0).astype(out.dtype)
    out[:, 2 * UNITS :] = dot(cotangent, p_down[...], 1, 0).astype(out.dtype)


def send_kernel(place, norms, held, c0, c1, c2, c3, out, p_gate, p_up, p_down, rows, done):
    copies = fetched(1 - lax.rem(place[0], 2), (c0, c1, c2, c3), rows, done)
    norm_sq = jnp.sum(norms[...], axis=0)[0:1, 0:1]
    scale = 0.7 * math.sqrt(3.0 * FF) / jnp.sqrt(norm_sq)
    for k, pert in enumerate((p_gate, p_up, p_down)):
        pert[...] = (held[k].astype(f32) + scale * held[3 + k].astype(f32)).astype(bf16)
    for copy in copies:
        copy.wait()
    products(rows, p_gate, p_up, p_down, out)


def keep_kernel(place, c0, c1, c2, c3, p_gate, p_up, p_down, out, rows, done):
    for copy in fetched(lax.rem(place[0], 2), (c0, c1, c2, c3), rows, done):
        copy.wait()
    products(rows, p_gate, p_up, p_down, out)


def hidden_kernel(parts, copies, hidden):
    def total(which):
        low = which * UNITS
        acc = parts[0, :, low : low + UNITS].astype(f32)
        for k in range(1, 4):
            acc = acc + parts[k, :, low : low + UNITS].astype(f32)
        return acc

    gate, upward, d_hidden = total(0), total(1), total(2)
    square = gate * gate
    bend = jnp.tanh(GELU_A * (gate + GELU_B * (gate * square)))
    half = 0.5 * (1.0 + bend)
    active = gate * half
    slope = half + 0.5 * gate * (1.0 - bend * bend) * (GELU_A * (1.0 + 3.0 * GELU_B * square))
    hidden[...] = (active * upward).astype(bf16)
    d_gate = (d_hidden * upward * slope).astype(bf16)
    d_up = (d_hidden * active).astype(bf16)
    for k in range(4):
        copies[k, :, 0:UNITS] = d_gate
        copies[k, :, UNITS:] = d_up


def tokens_kernel(flip, place, rows, p_gate, p_up, *rest):
    out = rest[-1]
    core = lax.rem(place[0], 2)
    half = 1 - core if flip else core
    value = dot(rows[:, 0:UNITS], p_gate[...], 1, 1)
    value = value + dot(rows[:, UNITS:], p_up[...], 1, 1)
    value = value.astype(bf16)
    for side in range(2):

        @pl.when(half == side)
        def store(low=side * WIDTH):
            for k in range(4):
                target = lax.rem(lax.div(place[0], 8) + k, 4)
                out[target, :, low : low + WIDTH] = value[k * ROWS : (k + 1) * ROWS]


def weights_kernel(place, c0, c1, c2, c3, own, other, grad_gate, grad_up, turned, rows, done):
    copies = []
    for k, chunk in enumerate((c0, c1, c2, c3)):
        target = rows.at[pl.ds(2 * k * ROWS, 2 * ROWS), :]
        copies.append(pltpu.make_async_copy(chunk, target, done.at[k]))
    for copy in copies:
        copy.start()
    for copy in copies:
        copy.wait()
    core = lax.rem(place[0], 2)
    tokens = []
    for half in (core, 1 - core):
        for k in range(4):
            start = pl.multiple_of(2 * k * ROWS + half * ROWS, ROWS)
            tokens.append(rows[pl.ds(start, ROWS), 0:WIDTH])
    tokens = jnp.concatenate(tokens, axis=0)
    moved = jnp.concatenate([own[...], other[...]], axis=0)
    grad_gate[...] = dot(tokens, moved[:, 0:UNITS], 0, 0).astype(bf16)
    grad_up[...] = dot(tokens, moved[:, UNITS:], 0, 0).astype(bf16)
    y = lax.div(lax.rem(place[0], 8), 2)
    for k in range(4):
        start = pl.multiple_of(lax.rem(y + k, 4) * 2 * ROWS, 2 * ROWS)
        turned[2 * k * ROWS : 2 * (k + 1) * ROWS, :] = rows[pl.ds(start, 2 * ROWS), PADDED : PADDED + WIDTH]


def down_kernel(cotangent, h0, h1, h2, h3, grad_down):
    hidden = jnp.concatenate([h0[...], h1[...], h2[...], h3[...]], axis=0)
    grad_down[...] = dot(cotangent[...], hidden, 0, 0).astype(bf16)


def body(tokens, w_gate, w_up, w_down, g_gate, g_up, g_down, cotangent):
    w_down, g_down = w_down.T, g_down.T
    place = 8 * lax.axis_index("dp") + 2 * lax.axis_index("y") + lax.axis_index("core")
    place = place.astype(jnp.int32).reshape(1)
    first = (tokens, cotangent, g_gate, g_up, g_down)
    packed = pl.pallas_call(
        pack_kernel,
        grid=(1,),
        out_shape=shape((8, 2 * PADDED)),
        in_specs=[whole_spec(x) for x in first],
        out_specs=vmem_spec(),
        compiler_params=pltpu.CompilerParams(vmem_limit_bytes=58 * 1024 * 1024),
        cost_estimate=pl.CostEstimate(flops=6 * WIDTH * UNITS, bytes_accessed=6 * WIDTH * UNITS, transcendentals=0),
    )(*first)
    mine = lax.all_gather(packed, "col", axis=0, tiled=True)
    chunks = [mine] + [
        lax.ppermute(mine, "dp", [(i, (i - k) % 4) for i in range(4)]) for k in (1, 2, 3)
    ]
    (norm,) = kernel_call(spread_kernel, [shape((32, 8, 128), f32)], (mine,), 128 * 128)
    norms = lax.all_to_all(norm, ("dp", "y", "core"), 0, 0, tiled=True)
    mult = 512 * WIDTH * UNITS * 2
    loaded = (norm, w_gate, w_up, w_down, g_gate, g_up, g_down)
    (held,) = kernel_call(
        load_kernel,
        [shape((6, WIDTH, UNITS))],
        loaded,
        0,
        [pl.BlockSpec(memory_space=pl.ANY)] + [whole_spec(x) for x in loaded[1:]],
        (1,),
    )
    anywhere = [pl.BlockSpec(memory_space=pl.ANY)] * 4
    fetch = [pltpu.VMEM((4 * ROWS, 2 * PADDED), bf16), pltpu.SemaphoreType.DMA((4,))]
    send, *perturbed = kernel_call(
        send_kernel,
        [shape((4 * ROWS, 3 * UNITS))] + [shape((WIDTH, UNITS))] * 3,
        (place, norms, held, *chunks),
        3 * mult // 2,
        [smem_spec()] + [vmem_spec()] * 2 + anywhere,
        scratch=fetch,
    )
    (keep,) = kernel_call(
        keep_kernel,
        [shape((4 * ROWS, 3 * UNITS), f32)],
        (place, *chunks, *perturbed),
        3 * mult // 2,
        [smem_spec()] + anywhere + [vmem_spec()] * 3,
        scratch=fetch,
    )
    swap = [(0, 1), (1, 0)]
    received = lax.ppermute(send, "core", swap)
    partial = (keep + received.astype(f32)).astype(bf16).reshape(4, ROWS, 3 * UNITS)
    parts = lax.all_to_all(partial, "y", 0, 0, tiled=True)
    moved, hidden = kernel_call(
        hidden_kernel,
        [shape((4, ROWS, 2 * UNITS)), shape((ROWS, UNITS))],
        (parts,),
        30 * ROWS * UNITS,
    )
    own = lax.all_to_all(moved, "y", 0, 0, tiled=True).reshape(4 * ROWS, 2 * UNITS)
    other = lax.ppermute(own, "core", swap)
    pair = lax.all_gather(hidden, "core", axis=0, tiled=True)
    other, pair = lax.optimization_barrier((other, pair))
    (grad_parts,) = kernel_call(
        functools.partial(tokens_kernel, False),
        [shape((4, ROWS, 2 * WIDTH))],
        (place, own, perturbed[0], perturbed[1]),
        mult,
        [smem_spec()] + [vmem_spec()] * 3,
    )
    (grad_parts,) = kernel_call(
        functools.partial(tokens_kernel, True),
        [shape((4, ROWS, 2 * WIDTH))],
        (place, other, perturbed[0], perturbed[1], grad_parts),
        mult,
        [smem_spec()] + [vmem_spec()] * 4,
        aliases={4: 0},
    )
    arrived = lax.all_to_all(grad_parts, "dp", 0, 0, tiled=True)
    (line,) = kernel_call(line_kernel, [shape((2 * ROWS, WIDTH))], (arrived,), 4 * 128 * WIDTH)
    line, pair = lax.optimization_barrier((line, pair))
    pieces = lax.all_to_all(line.reshape(16, 8, WIDTH), "col", 0, 0, tiled=True)
    pairs = [pair] + [
        lax.ppermute(pair, "y", [(i, (i - k) % 4) for i in range(4)]) for k in (1, 2, 3)
    ]
    grad_gate, grad_up, turned = kernel_call(
        weights_kernel,
        [shape((WIDTH, UNITS))] * 2 + [shape((8 * ROWS, WIDTH))],
        (place, *chunks, own, other),
        2 * mult,
        [smem_spec()] + anywhere + [vmem_spec()] * 2,
        scratch=[pltpu.VMEM((8 * ROWS, 2 * PADDED), bf16), pltpu.SemaphoreType.DMA((4,))],
    )
    (grad_down,) = kernel_call(
        down_kernel,
        [shape((WIDTH, UNITS))],
        (turned, *pairs),
        mult,
    )
    (grad_tokens,) = kernel_call(sum_kernel, [shape((8, WIDTH))], (pieces,), 128 * WIDTH)
    return (grad_tokens, grad_gate, grad_up, grad_down.T)


def solution(mesh):
    fine = Mesh(mesh.devices.reshape(4, 4, 2, 16), ("dp", "y", "core", "col"))
    by_rows = P(("dp", "col"), ("y", "core"))
    by_columns = P(("y", "core"), ("dp", "col"))
    return jax.shard_map(
        body,
        mesh=fine,
        in_specs=(by_rows, by_columns, by_columns, by_rows, by_columns, by_columns, by_rows, by_rows),
        out_specs=(by_rows, by_columns, by_columns, by_rows),
        check_vma=False,
    )
```

```python
import functools
import math

import jax
import jax.numpy as jnp
from jax import lax
from jax.experimental import pallas as pl
from jax.experimental.pallas import tpu as pltpu
from jax.sharding import Mesh, PartitionSpec as P

FF = 24576
WIDTH = 576
UNITS = 384
ROWS = 64
PADDED = 640
bf16, f32 = jnp.bfloat16, jnp.float32
GELU_A = math.sqrt(2.0 / math.pi)
GELU_B = 0.044715
VMEM_BYTES = 16 * 1024 * 1024


def vmem_spec():
    return pl.BlockSpec(memory_space=pltpu.VMEM)


def smem_spec():
    return pl.BlockSpec(memory_space=pltpu.SMEM)


def kernel_call(kernel, outs, operands, flops, specs=None, grid=(), aliases=None, scratch=()):
    size = sum(x.size * x.dtype.itemsize for x in list(operands) + list(outs))
    return pl.pallas_call(
        kernel,
        grid=grid,
        out_shape=outs,
        scratch_shapes=scratch,
        input_output_aliases=aliases or {},
        in_specs=specs or [vmem_spec()] * len(operands),
        out_specs=[vmem_spec()] * len(outs),
        compiler_params=pltpu.CompilerParams(vmem_limit_bytes=VMEM_BYTES),
        cost_estimate=pl.CostEstimate(flops=flops, bytes_accessed=size, transcendentals=0),
    )(*operands)


def shape(dims, dtype=bf16):
    return jax.ShapeDtypeStruct(dims, dtype)


def whole_spec(x):
    return pl.BlockSpec(x.shape, lambda i: (0,) * len(x.shape))


def pack_kernel(tokens, cotangent, g_gate, g_up, g_down, out):
    total = jnp.zeros((16, UNITS), f32)
    for ref in (g_gate, g_up, g_down):
        for start in range(0, WIDTH, 16):
            part = ref[start : start + 16, :].astype(f32)
            total = total + part * part
    norm = jnp.sum(jnp.sum(total, axis=0, keepdims=True), axis=1, keepdims=True)
    high = norm.astype(bf16).astype(f32)
    middle = (norm - high).astype(bf16).astype(f32)
    low = norm - high - middle
    row = lax.broadcasted_iota(jnp.int32, (8, PADDED - WIDTH), 0)
    digits = jnp.where(row == 0, high, jnp.where(row == 1, middle, jnp.where(row == 2, low, 0.0)))
    out[:, 0:WIDTH] = tokens[...]
    out[:, WIDTH:PADDED] = digits.astype(bf16)
    out[:, PADDED : PADDED + WIDTH] = cotangent[...]
    out[:, PADDED + WIDTH :] = jnp.zeros((8, PADDED - WIDTH), bf16)


def spread_kernel(digits, out):
    block = digits[:, PADDED - 128 : PADDED].astype(f32)
    lane = lax.broadcasted_iota(jnp.int32, block.shape, 1)
    block = jnp.where(lane == 127, block, 0.0)
    total = jnp.sum(jnp.sum(block, axis=0, keepdims=True), axis=1, keepdims=True)
    out[...] = jnp.broadcast_to(total.reshape(1, 1, 1), out.shape)


def line_kernel(parts, out):
    total = parts[0].astype(f32)
    for k in range(1, 4):
        total = total + parts[k].astype(f32)
    out[0:ROWS, :] = total[:, 0:WIDTH].astype(bf16)
    out[ROWS:, :] = total[:, WIDTH:].astype(bf16)


def sum_kernel(parts, out):
    width = out.shape[1]
    total = parts[0, :, 0:width].astype(f32)
    for k in range(1, parts.shape[0]):
        total = total + parts[k, :, 0:width].astype(f32)
    out[...] = total.astype(bf16)


def dot(left, right, left_dim, right_dim):
    return lax.dot_general(
        left, right, (((left_dim,), (right_dim,)), ((), ())), preferred_element_type=f32
    )


def load_kernel(after, w_gate, w_up, w_down, g_gate, g_up, g_down, held):
    del after
    for k, ref in enumerate((w_gate, w_up, w_down, g_gate, g_up, g_down)):
        held[k] = ref[...]


def fetched(half, chunks, rows, done, base=0):
    start = pl.multiple_of(half * ROWS, ROWS)
    copies = []
    for k, chunk in enumerate(chunks):
        source = chunk.at[pl.ds(start, ROWS), :]
        target = rows.at[pl.ds((base + k) * ROWS, ROWS), :]
        copies.append(pltpu.make_async_copy(source, target, done.at[base + k]))
    for copy in copies:
        copy.start()
    return copies


def products(rows, p_gate, p_up, p_down, out):
    tokens = rows[:, 0:WIDTH]
    cotangent = rows[:, PADDED : PADDED + WIDTH]
    out[:, 0:UNITS] = dot(tokens, p_gate[...], 1, 0).astype(out.dtype)
    out[:, UNITS : 2 * UNITS] = dot(tokens, p_up[...], 1, 0).astype(out.dtype)
    out[:, 2 * UNITS :] = dot(cotangent, p_down[...], 1, 0).astype(out.dtype)


def send_kernel(place, norms, held, c0, c1, c2, c3, out, p_gate, p_up, p_down, rows, done):
    copies = fetched(1 - lax.rem(place[0], 2), (c0, c1, c2, c3), rows, done)
    norm_sq = jnp.sum(norms[...], axis=0)[0:1, 0:1]
    scale = 0.7 * math.sqrt(3.0 * FF) / jnp.sqrt(norm_sq)
    for k, pert in enumerate((p_gate, p_up, p_down)):
        pert[...] = (held[k].astype(f32) + scale * held[3 + k].astype(f32)).astype(bf16)
    for copy in copies:
        copy.wait()
    products(rows, p_gate, p_up, p_down, out)


def keep_kernel(place, c0, c1, c2, c3, p_gate, p_up, p_down, out, rows, done):
    for copy in fetched(lax.rem(place[0], 2), (c0, c1, c2, c3), rows, done):
        copy.wait()
    products(rows, p_gate, p_up, p_down, out)


def hidden_kernel(parts, copies, hidden):
    def total(which):
        low = which * UNITS
        acc = parts[0, :, low : low + UNITS].astype(f32)
        for k in range(1, 4):
            acc = acc + parts[k, :, low : low + UNITS].astype(f32)
        return acc

    gate, upward, d_hidden = total(0), total(1), total(2)
    square = gate * gate
    bend = jnp.tanh(GELU_A * (gate + GELU_B * (gate * square)))
    half = 0.5 * (1.0 + bend)
    active = gate * half
    slope = half + 0.5 * gate * (1.0 - bend * bend) * (GELU_A * (1.0 + 3.0 * GELU_B * square))
    hidden[...] = (active * upward).astype(bf16)
    d_gate = (d_hidden * upward * slope).astype(bf16)
    d_up = (d_hidden * active).astype(bf16)
    for k in range(4):
        copies[k, :, 0:UNITS] = d_gate
        copies[k, :, UNITS:] = d_up


def tokens_kernel(flip, place, rows, p_gate, p_up, *rest):
    out = rest[-1]
    core = lax.rem(place[0], 2)
    half = 1 - core if flip else core
    value = dot(rows[:, 0:UNITS], p_gate[...], 1, 1)
    value = value + dot(rows[:, UNITS:], p_up[...], 1, 1)
    value = value.astype(bf16)
    for side in range(2):

        @pl.when(half == side)
        def store(low=side * WIDTH):
            for k in range(4):
                target = lax.rem(lax.div(place[0], 8) + k, 4)
                out[target, :, low : low + WIDTH] = value[k * ROWS : (k + 1) * ROWS]


def weights_kernel(place, c0, c1, c2, c3, own, other, grad_gate, grad_up, turned, rows, done):
    copies = []
    for k, chunk in enumerate((c0, c1, c2, c3)):
        target = rows.at[pl.ds(2 * k * ROWS, 2 * ROWS), :]
        copies.append(pltpu.make_async_copy(chunk, target, done.at[k]))
    for copy in copies:
        copy.start()
    for copy in copies:
        copy.wait()
    core = lax.rem(place[0], 2)
    tokens = []
    for half in (core, 1 - core):
        for k in range(4):
            start = pl.multiple_of(2 * k * ROWS + half * ROWS, ROWS)
            tokens.append(rows[pl.ds(start, ROWS), 0:WIDTH])
    tokens = jnp.concatenate(tokens, axis=0)
    moved = jnp.concatenate([own[...], other[...]], axis=0)
    grad_gate[...] = dot(tokens, moved[:, 0:UNITS], 0, 0).astype(bf16)
    grad_up[...] = dot(tokens, moved[:, UNITS:], 0, 0).astype(bf16)
    y = lax.div(lax.rem(place[0], 8), 2)
    for k in range(4):
        start = pl.multiple_of(lax.rem(y + k, 4) * 2 * ROWS, 2 * ROWS)
        turned[2 * k * ROWS : 2 * (k + 1) * ROWS, :] = rows[pl.ds(start, 2 * ROWS), PADDED : PADDED + WIDTH]


def down_kernel(cotangent, h0, h1, h2, h3, grad_down):
    hidden = jnp.concatenate([h0[...], h1[...], h2[...], h3[...]], axis=0)
    grad_down[...] = dot(cotangent[...], hidden, 0, 0).astype(bf16)


def body(tokens, w_gate, w_up, w_down, g_gate, g_up, g_down, cotangent):
    w_down, g_down = w_down.T, g_down.T
    place = 8 * lax.axis_index("dp") + 2 * lax.axis_index("y") + lax.axis_index("core")
    place = place.astype(jnp.int32).reshape(1)
    first = (tokens, cotangent, g_gate, g_up, g_down)
    packed = pl.pallas_call(
        pack_kernel,
        grid=(1,),
        out_shape=shape((8, 2 * PADDED)),
        in_specs=[whole_spec(x) for x in first],
        out_specs=vmem_spec(),
        compiler_params=pltpu.CompilerParams(vmem_limit_bytes=58 * 1024 * 1024),
        cost_estimate=pl.CostEstimate(flops=6 * WIDTH * UNITS, bytes_accessed=6 * WIDTH * UNITS, transcendentals=0),
    )(*first)
    mine = lax.all_gather(packed, "col", axis=0, tiled=True)
    chunks = [mine] + [
        lax.ppermute(mine, "dp", [(i, (i - k) % 4) for i in range(4)]) for k in (1, 2, 3)
    ]
    (norm,) = kernel_call(spread_kernel, [shape((32, 1, 128), f32)], (mine,), 128 * 128)
    norms = lax.all_to_all(norm, ("dp", "y", "core"), 0, 0, tiled=True)
    mult = 512 * WIDTH * UNITS * 2
    loaded = (norm, w_gate, w_up, w_down, g_gate, g_up, g_down)
    (held,) = kernel_call(
        load_kernel,
        [shape((6, WIDTH, UNITS))],
        loaded,
        0,
        [pl.BlockSpec(memory_space=pl.ANY)] + [whole_spec(x) for x in loaded[1:]],
        (1,),
    )
    anywhere = [pl.BlockSpec(memory_space=pl.ANY)] * 4
    fetch = [pltpu.VMEM((4 * ROWS, 2 * PADDED), bf16), pltpu.SemaphoreType.DMA((4,))]
    send, *perturbed = kernel_call(
        send_kernel,
        [shape((4 * ROWS, 3 * UNITS))] + [shape((WIDTH, UNITS))] * 3,
        (place, norms, held, *chunks),
        3 * mult // 2,
        [smem_spec()] + [vmem_spec()] * 2 + anywhere,
        scratch=fetch,
    )
    (keep,) = kernel_call(
        keep_kernel,
        [shape((4 * ROWS, 3 * UNITS), f32)],
        (place, *chunks, *perturbed),
        3 * mult // 2,
        [smem_spec()] + anywhere + [vmem_spec()] * 3,
        scratch=fetch,
    )
    swap = [(0, 1), (1, 0)]
    received = lax.ppermute(send, "core", swap)
    partial = (keep + received.astype(f32)).astype(bf16).reshape(4, ROWS, 3 * UNITS)
    parts = lax.all_to_all(partial, "y", 0, 0, tiled=True)
    moved, hidden = kernel_call(
        hidden_kernel,
        [shape((4, ROWS, 2 * UNITS)), shape((ROWS, UNITS))],
        (parts,),
        30 * ROWS * UNITS,
    )
    own = lax.all_to_all(moved, "y", 0, 0, tiled=True).reshape(4 * ROWS, 2 * UNITS)
    other = lax.ppermute(own, "core", swap)
    pair = lax.all_gather(hidden, "core", axis=0, tiled=True)
    other, pair = lax.optimization_barrier((other, pair))
    (grad_parts,) = kernel_call(
        functools.partial(tokens_kernel, False),
        [shape((4, ROWS, 2 * WIDTH))],
        (place, own, perturbed[0], perturbed[1]),
        mult,
        [smem_spec()] + [vmem_spec()] * 3,
    )
    (grad_parts,) = kernel_call(
        functools.partial(tokens_kernel, True),
        [shape((4, ROWS, 2 * WIDTH))],
        (place, other, perturbed[0], perturbed[1], grad_parts),
        mult,
        [smem_spec()] + [vmem_spec()] * 4,
        aliases={4: 0},
    )
    arrived = lax.all_to_all(grad_parts, "dp", 0, 0, tiled=True)
    (line,) = kernel_call(line_kernel, [shape((2 * ROWS, WIDTH))], (arrived,), 4 * 128 * WIDTH)
    line, pair = lax.optimization_barrier((line, pair))
    pieces = lax.all_to_all(line.reshape(16, 8, WIDTH), "col", 0, 0, tiled=True)
    pairs = [pair] + [
        lax.ppermute(pair, "y", [(i, (i - k) % 4) for i in range(4)]) for k in (1, 2, 3)
    ]
    grad_gate, grad_up, turned = kernel_call(
        weights_kernel,
        [shape((WIDTH, UNITS))] * 2 + [shape((8 * ROWS, WIDTH))],
        (place, *chunks, own, other),
        2 * mult,
        [smem_spec()] + anywhere + [vmem_spec()] * 2,
        scratch=[pltpu.VMEM((8 * ROWS, 2 * PADDED), bf16), pltpu.SemaphoreType.DMA((4,))],
    )
    (grad_down,) = kernel_call(
        down_kernel,
        [shape((WIDTH, UNITS))],
        (turned, *pairs),
        mult,
    )
    (grad_tokens,) = kernel_call(sum_kernel, [shape((8, WIDTH))], (pieces,), 128 * WIDTH)
    return (grad_tokens, grad_gate, grad_up, grad_down.T)


def solution(mesh):
    fine = Mesh(mesh.devices.reshape(4, 4, 2, 16), ("dp", "y", "core", "col"))
    by_rows = P(("dp", "col"), ("y", "core"))
    by_columns = P(("y", "core"), ("dp", "col"))
    return jax.shard_map(
        body,
        mesh=fine,
        in_specs=(by_rows, by_columns, by_columns, by_rows, by_columns, by_columns, by_rows, by_rows),
        out_specs=(by_rows, by_columns, by_columns, by_rows),
        check_vma=False,
    )
```
